256 devices in a mesh: section: 4 (over x), tensor: 16 (over z_hi, y), dp: 4 (over z_lo, core).
Axes of the slice: x: 4, y: 4, z: 8 (z_hi: 4, z_lo: 2; z = z_hi * 2 + z_lo), core: 2. Of those that a mesh axis runs over, the one named last changes fastest.
Arguments:
- first_inputs: bfloat16 [4, 256, 8192], P('section', 'tensor', 'dp'), may hold values from -24 to 24
- new_batch: bfloat16 [256, 8192], P('tensor', 'dp'), may hold values from -24 to 24
- stashed: bfloat16 [2, 4, 256, 8192], P(None, 'section', 'tensor', 'dp'), may hold values from -24 to 24
- first_grads: bfloat16 [4, 256, 8192], P('section', 'tensor', 'dp'), may hold values from -24 to 24
- new_grads: bfloat16 [256, 8192], P('tensor', 'dp'), may hold values from -24 to 24
- gains: float32 [4, 8192], P('section', 'dp'), may hold values from 0.25 to 1.75
- up_weights: bfloat16 [4, 8192, 16384], P('section', 'dp', 'tensor'), may hold values from -0.0625 to 0.0625
- down_weights: bfloat16 [4, 16384, 8192], P('section', 'tensor', 'dp'), may hold values from -0.046875 to 0.046875
Outputs:
- activations: bfloat16 [2, 4, 256, 8192], P(None, 'section', 'tensor', 'dp')
- input_grads: bfloat16 [2, 4, 256, 8192], P(None, 'section', 'tensor', 'dp')
The draws below stay inside these ranges and needn't reach their ends.
All inputs are finite; a program needn't handle non-finite values.
Results may differ from the reference program's by a relative error of at most 0.0051.
Values may be sent and summed in bfloat16 or wider, within the bound.
No kernel may reach another device: no remote copies, remote signals or barrier semaphores. Data moves between devices by JAX's collectives and lax.ppermute only.
A program may use at most 64 MiB of HBM per device.

```python
import jax
import jax.numpy as jnp
from jax import lax

D = 8192
H = 16384
TOK = 256
SECTIONS = 4


def activation_law(key, shape, row_top):
    noise_key, channel_key, offset_key, row_key = jax.random.split(key, 4)
    columns = shape[-1]
    rising = jnp.exp(jnp.log(3.0) * jnp.arange(columns, dtype=jnp.float32) / columns)
    rough = jax.random.uniform(channel_key, (columns,), jnp.float32, 0.5, 1.5)
    offset = jax.random.uniform(offset_key, (columns,), jnp.float32, -0.8, 0.8)
    noise = jnp.clip(jax.random.normal(noise_key, shape, jnp.float32), -4.0, 4.0)
    row_scale = jnp.exp(jax.random.uniform(row_key, shape[:-1] + (1,), jnp.float32, 0.0, jnp.log(row_top)))
    return (0.5 * (noise + offset) * rough * rising * row_scale).astype(jnp.bfloat16)


def draw_first_inputs(key, part):
    key = jax.random.fold_in(key, 11)
    row_top = 1.0
    return activation_law(key, (SECTIONS, TOK, D), row_top)


def draw_new_batch(key, part):
    key = jax.random.fold_in(key, 12)
    row_top = 1.0
    return activation_law(key, (TOK, D), row_top)


def draw_stashed(key, part):
    key = jax.random.fold_in(key, 13)
    row_top = 1.0
    return activation_law(key, (2, SECTIONS, TOK, D), row_top)


def draw_first_grads(key, part):
    key = jax.random.fold_in(key, 14)
    row_top = 1.0
    return activation_law(key, (SECTIONS, TOK, D), row_top)


def draw_new_grads(key, part):
    key = jax.random.fold_in(key, 15)
    row_top = 1.0
    return activation_law(key, (TOK, D), row_top)


def level_of(key, dims, pieces, least, largest):
    def one(axis_at, blocks):
        steps = jax.random.uniform(jax.random.fold_in(jax.random.fold_in(key, 6), axis_at), (blocks,), jnp.float32, least / len(pieces), largest / len(pieces))
        return jnp.repeat(jnp.exp(steps), dims[axis_at] // blocks).reshape((-1,) + (1,) * (len(dims) - axis_at - 1))

    level = one(*pieces[0])
    for cut in pieces[1:]:
        level = level * one(*cut)
    return level


def bell_draw(rng, extent, scale, limit, cuts=(), held_as=jnp.bfloat16):
    array = scale * jax.random.normal(rng, extent, jnp.float32)
    if cuts:
        array = array * level_of(rng, extent, cuts, -0.22, 0.18)
    return jnp.clip(array, -limit, limit).astype(held_as)


def setup_inputs(seed: int = 0) -> dict:
    key_list = jax.random.split(jax.random.key(seed), 9)
    first_inputs = draw_first_inputs(jax.random.fold_in(key_list[8], 71), 0)
    new_batch = draw_new_batch(jax.random.fold_in(key_list[8], 71), 0)
    stashed = draw_stashed(jax.random.fold_in(key_list[8], 71), 0)
    first_grads = draw_first_grads(jax.random.fold_in(key_list[8], 71), 0)
    new_grads = draw_new_grads(jax.random.fold_in(key_list[8], 71), 0)
    gains = jnp.clip(1.0 + 0.15 * jax.random.normal(key_list[5], (SECTIONS, D), jnp.float32), 0.25, 1.75)
    up_weights = bell_draw(key_list[6], (SECTIONS, D, H), D ** -0.5, 0.0625, ((0, 4), (1, 4), (2, 16)))
    down_weights = bell_draw(key_list[7], (SECTIONS, H, D), H ** -0.5, 0.046875, ((0, 4), (1, 16), (2, 4)))
    return dict(first_inputs=first_inputs, new_batch=new_batch, stashed=stashed, first_grads=first_grads, new_grads=new_grads, gains=gains, up_weights=up_weights, down_weights=down_weights)


EPSILON = 1e-05
SLOPE = 0.7978845608028654
CUBIC = 0.044715
CONTRACT = (((1,), (1,)), ((), ()))

def gelu_value(preact):
    return 0.5 * preact * (1.0 + jnp.tanh(SLOPE * (preact + CUBIC * preact * preact * preact)))

def gelu_slope(preact):
    tangent = jnp.tanh(SLOPE * (preact + CUBIC * preact * preact * preact))
    return 0.5 * (1.0 + tangent) + 0.5 * preact * (1.0 - tangent * tangent) * SLOPE * (1.0 + 3.0 * CUBIC * preact * preact)

def normalize(layer_in, gain_row):
    wide = layer_in.astype(jnp.float32)
    average = lax.optimization_barrier(jnp.sum(wide, axis=-1, keepdims=True)) / D
    inverse_scale = lax.rsqrt(lax.optimization_barrier(jnp.sum(wide * wide, axis=-1, keepdims=True)) / D - average * average + EPSILON)
    normed = (wide - average) * inverse_scale
    return (wide, normed, inverse_scale, (normed * gain_row).astype(jnp.bfloat16))

def layer_forward(layer_in, gain_row, up_matrix, down_matrix):
    parts = normalize(layer_in, gain_row)
    preact = jnp.dot(parts[3], up_matrix, preferred_element_type=jnp.float32)
    active = gelu_value(preact).astype(jnp.bfloat16)
    result = parts[0] + jnp.dot(active, down_matrix, preferred_element_type=jnp.float32)
    return result.astype(jnp.bfloat16)

def layer_backward(layer_in, out_grad, gain_row, up_matrix, down_matrix):
    parts = normalize(layer_in, gain_row)
    preact = jnp.dot(parts[3], up_matrix, preferred_element_type=jnp.float32)
    upstream = lax.dot_general(out_grad, down_matrix, CONTRACT, preferred_element_type=jnp.float32)
    slopes = (upstream * gelu_slope(preact)).astype(jnp.bfloat16)
    grad_hidden = lax.dot_general(slopes, up_matrix, CONTRACT, preferred_element_type=jnp.float32)
    grad_normed = grad_hidden * gain_row
    grad_mean = lax.optimization_barrier(jnp.sum(grad_normed, axis=-1, keepdims=True)) / D
    grad_cross = lax.optimization_barrier(jnp.sum(grad_normed * parts[1], axis=-1, keepdims=True)) / D
    result = out_grad.astype(jnp.float32) + parts[2] * (grad_normed - grad_mean - parts[1] * grad_cross)
    return result.astype(jnp.bfloat16)

def reference(first_inputs, new_batch, stashed, first_grads, new_grads, gains, up_weights, down_weights):
    early_out = []
    early_grad = []
    for section_index in range(SECTIONS):
        early_out.append(layer_forward(first_inputs[section_index], gains[section_index], up_weights[section_index], down_weights[section_index]))
        early_grad.append(layer_backward(stashed[0, section_index], first_grads[section_index], gains[section_index], up_weights[section_index], down_weights[section_index]))
    later_out = []
    later_grad = []
    for section_index in range(SECTIONS):
        entering = new_batch if section_index == 0 else early_out[section_index - 1]
        incoming = new_grads if section_index == SECTIONS - 1 else early_grad[section_index + 1]
        later_out.append(layer_forward(entering, gains[section_index], up_weights[section_index], down_weights[section_index]))
        later_grad.append(layer_backward(stashed[1, section_index], incoming, gains[section_index], up_weights[section_index], down_weights[section_index]))
    activations = jnp.stack([jnp.stack(early_out), jnp.stack(later_out)])
    input_grads = jnp.stack([jnp.stack(early_grad), jnp.stack(later_grad)])
    return (activations, input_grads)
```

```python
import jax
import jax.numpy as jnp
from jax import lax
from jax.sharding import PartitionSpec as P

D = 8192
EPSILON = 1e-05
SLOPE = 0.7978845608028654
CUBIC = 0.044715
CONTRACT = (((1,), (1,)), ((), ()))
BF = jnp.bfloat16
F32 = jnp.float32

PLANE = ("tensor", "dp")


def place(z_hi, y, z_lo, core):
    return ((z_hi * 4 + y) * 2 + z_lo) * 2 + core


def partner(i, k):
    return i ^ 1 if k == 0 else ((i + 1) % 4 if i % 2 else (i - 1) % 4)


def plane_pairs(rule):
    return [
        (place(z, y, w, c), place(*rule(z, y, w, c)))
        for z in range(4)
        for y in range(4)
        for w in range(2)
        for c in range(2)
    ]


Y_STEPS = [plane_pairs(lambda z, y, w, c, k=k: (z, partner(y, (k + c) % 2), w, c)) for k in range(2)]
Z_STEPS = [plane_pairs(lambda z, y, w, c, k=k: (partner(z, (k + c) % 2), y, w, c)) for k in range(2)]
ACROSS_Z = plane_pairs(lambda z, y, w, c: (z, y, 1 - w, c))
ACROSS_CORE = plane_pairs(lambda z, y, w, c: (z, y, w, 1 - c))


def swap(value, pairs):
    return lax.ppermute(value, PLANE, pairs)


def passed_along(value, by):
    pairs = [(i, i + by) for i in range(4) if 0 <= i + by < 4]
    return lax.ppermute(value, "section", pairs)


def gelu_value(preact):
    return 0.5 * preact * (1.0 + jnp.tanh(SLOPE * (preact + CUBIC * preact * preact * preact)))


def gelu_slope(preact):
    tangent = jnp.tanh(SLOPE * (preact + CUBIC * preact * preact * preact))
    return 0.5 * (1.0 + tangent) + 0.5 * preact * (1.0 - tangent * tangent) * SLOPE * (
        1.0 + 3.0 * CUBIC * preact * preact
    )


def rows(*parts):
    return jnp.concatenate(parts, axis=0)


def gather(block):
    for pairs in Z_STEPS:
        block = rows(block, swap(block, pairs))
    block = rows(block, swap(block, Y_STEPS[0]))
    return block, swap(block, Y_STEPS[1])


def scatter_sum(near, far):
    total = near + swap(far.astype(BF), Y_STEPS[1]).astype(F32)
    for pairs in (Y_STEPS[0], Z_STEPS[1], Z_STEPS[0]):
        half = total.shape[0] // 2
        total = total[:half] + swap(total[half:].astype(BF), pairs).astype(F32)
    return total


def moments(wide):
    return jnp.concatenate(
        [jnp.sum(wide, axis=-1, keepdims=True), jnp.sum(wide * wide, axis=-1, keepdims=True)], axis=-1
    )


def both_z(partial):
    return partial + swap(partial, ACROSS_Z)


def normalize(wide, sums, gain):
    average = sums[:, :1] / D
    inverse_scale = lax.rsqrt(sums[:, 1:2] / D - average * average + EPSILON)
    normed = (wide - average) * inverse_scale
    return normed, inverse_scale, (normed * gain).astype(BF)


def wide_dot(left, pair, dims):
    half = left.shape[1] // 2
    return lax.dot_general(left[:, :half], pair[0], dims, preferred_element_type=F32) + lax.dot_general(
        left[:, half:], pair[1], dims, preferred_element_type=F32
    )


def spread_dot(left, pair, dims):
    return jnp.concatenate(
        [lax.dot_general(left, m, dims, preferred_element_type=F32) for m in pair], axis=1
    )


PLAIN = (((1,), (0,)), ((), ()))


def across(part):
    return part + swap(part.astype(BF), ACROSS_Z).astype(F32)


def split_pair(gathered):
    blocks = gathered.reshape(-1, 2, 8, gathered.shape[1])
    return [blocks[:, i].reshape(-1, gathered.shape[1]) for i in range(2)]


def forward(wide, normed_rows, up, down):
    halves = gather(normed_rows)
    terms = []
    for half in halves:
        active = gelu_value(across(wide_dot(half, up, PLAIN))).astype(BF)
        terms.append(spread_dot(active, down, PLAIN))
    return (wide + scatter_sum(*terms)).astype(BF)


def preacts(rows_halves, up):
    return [across(wide_dot(half, up, PLAIN)) for half in rows_halves]


def backward_tail(preact_halves, grad_halves, grad, normed, inverse_scale, gain, up):
    terms = []
    for preact, upstream in zip(preact_halves, grad_halves):
        slopes = (upstream * gelu_slope(preact)).astype(BF)
        terms.append(spread_dot(slopes, up, CONTRACT))
    grad_normed = scatter_sum(*terms) * gain
    sums = both_z(
        jnp.concatenate(
            [
                jnp.sum(grad_normed, axis=-1, keepdims=True),
                jnp.sum(grad_normed * normed, axis=-1, keepdims=True),
            ],
            axis=-1,
        )
    ) / D
    result = grad.astype(F32) + inverse_scale * (grad_normed - sums[:, :1] - normed * sums[:, 1:2])
    return result.astype(BF)


def shards(
    first_inputs, new_batch, stashed, first_grads, new_grads, gains, up_weights, down_weights
):
    core = lax.axis_index("dp") % 2
    section = lax.axis_index("section")

    mine = jnp.stack([first_inputs[0], stashed[0, 0], first_grads[0], stashed[1, 0], new_batch, new_grads])
    kept = lax.dynamic_slice_in_dim(mine, core * 8, 8, axis=1)
    given = lax.dynamic_slice_in_dim(mine, (1 - core) * 8, 8, axis=1)
    inputs = jnp.concatenate([kept, swap(given, ACROSS_CORE)], axis=2)
    first_in, first_stash, first_grad, second_stash, fresh_in, fresh_grad = inputs
    gain = jnp.concatenate([gains, swap(gains, ACROSS_CORE)], axis=1)
    up = (up_weights[0], swap(up_weights[0], ACROSS_CORE))
    down = (down_weights[0], swap(down_weights[0], ACROSS_CORE))

    wides = [x.astype(F32) for x in (first_in, first_stash, second_stash)]
    sums = both_z(jnp.concatenate([moments(w) for w in wides], axis=-1))
    _, _, forward_rows = normalize(wides[0], sums[:, 0:2], gain)
    normed, inverse_scale, backward_rows = normalize(wides[1], sums[:, 2:4], gain)
    normed_2, inverse_scale_2, backward_rows_2 = normalize(wides[2], sums[:, 4:6], gain)

    pairs = [split_pair(half) for half in gather(rows(backward_rows, first_grad))]
    preact_halves, grad_halves = [], []
    for normed_half, grad_half in pairs:
        both = across(jnp.stack([wide_dot(normed_half, up, PLAIN), wide_dot(grad_half, down, CONTRACT)]))
        preact_halves.append(both[0])
        grad_halves.append(both[1])
    early_out = forward(wides[0], forward_rows, up, down)
    early_grad = backward_tail(preact_halves, grad_halves, first_grad, normed, inverse_scale, gain, up)
    preact_halves_2 = preacts(gather(backward_rows_2), up)

    later_incoming = jnp.where(section == 3, fresh_grad, passed_along(early_grad, -1))
    later_input = jnp.where(section == 0, fresh_in, passed_along(early_out, 1))
    wide = later_input.astype(F32)
    _, _, forward_rows_2 = normalize(wide, both_z(moments(wide)), gain)
    grad_halves_2 = [across(wide_dot(half, down, CONTRACT)) for half in gather(later_incoming)]
    later_out = forward(wide, forward_rows_2, up, down)
    later_grad = backward_tail(
        preact_halves_2, grad_halves_2, later_incoming, normed_2, inverse_scale_2, gain, up
    )

    def returned(early, later):
        both = jnp.stack([early, later])
        here = both[:, :, :2048]
        there = swap(both[:, :, 2048:], ACROSS_CORE)
        low = jnp.where(core == 0, here, there)
        high = jnp.where(core == 0, there, here)
        return jnp.concatenate([low, high], axis=1)[:, None]

    return returned(early_out, later_out), returned(early_grad, later_grad)


def solution(mesh):
    return jax.shard_map(
        shards,
        mesh=mesh,
        in_specs=(
            P("section", "tensor", "dp"),
            P("tensor", "dp"),
            P(None, "section", "tensor", "dp"),
            P("section", "tensor", "dp"),
            P("tensor", "dp"),
            P("section", "dp"),
            P("section", "dp", "tensor"),
            P("section", "tensor", "dp"),
        ),
        out_specs=(P(None, "section", "tensor", "dp"), P(None, "section", "tensor", "dp")),
        check_vma=False,
    )
```

```python
import functools

import jax
import jax.numpy as jnp
from jax import lax
from jax.experimental import pallas as pl
from jax.experimental.pallas import tpu as pltpu
from jax.sharding import PartitionSpec as P

D = 8192
EPSILON = 1e-05
SLOPE = 0.7978845608028654
CUBIC = 0.044715
CONTRACT = (((1,), (1,)), ((), ()))
BF = jnp.bfloat16
F32 = jnp.float32

PLANE = ("tensor", "dp")


def place(z_hi, y, z_lo, core):
    return ((z_hi * 4 + y) * 2 + z_lo) * 2 + core


def partner(i, k):
    return i ^ 1 if k == 0 else ((i + 1) % 4 if i % 2 else (i - 1) % 4)


def plane_pairs(rule):
    return [
        (place(z, y, w, c), place(*rule(z, y, w, c)))
        for z in range(4)
        for y in range(4)
        for w in range(2)
        for c in range(2)
    ]


Y_STEPS = [plane_pairs(lambda z, y, w, c, k=k: (z, partner(y, (k + c) % 2), w, c)) for k in range(2)]
Z_STEPS = [plane_pairs(lambda z, y, w, c, k=k: (partner(z, (k + c) % 2), y, w, c)) for k in range(2)]
ACROSS_Z = plane_pairs(lambda z, y, w, c: (z, y, 1 - w, c))
ACROSS_CORE = plane_pairs(lambda z, y, w, c: (z, y, w, 1 - c))


def swap(value, pairs):
    return lax.ppermute(value, PLANE, pairs)


def gelu_value(preact):
    return 0.5 * preact * (1.0 + jnp.tanh(SLOPE * (preact + CUBIC * preact * preact * preact)))


def gelu_slope(preact):
    tangent = jnp.tanh(SLOPE * (preact + CUBIC * preact * preact * preact))
    return 0.5 * (1.0 + tangent) + 0.5 * preact * (1.0 - tangent * tangent) * SLOPE * (
        1.0 + 3.0 * CUBIC * preact * preact
    )


def rows(*parts):
    return jnp.concatenate(parts, axis=0)


def after(value, *others):
    return lax.optimization_barrier((value, others))[0]


def gathering(block, steps):
    for pairs in steps:
        (other,) = yield [(block, pairs)]
        block = jnp.concatenate([block, other], axis=1)
    return block


def scattering(near, far, other_total):
    (other,) = yield [(far.astype(BF), Y_STEPS[1])]
    total = near + other.astype(F32)
    total = jnp.stack([jnp.pad(other_total, ((0, 0), (0, total.shape[1] - other_total.shape[1]))), total])
    for pairs in (Y_STEPS[0], Z_STEPS[1], Z_STEPS[0]):
        half = total.shape[1] // 2
        (other,) = yield [(total[:, half:].astype(BF), pairs)]
        total = total[:, :half] + other.astype(F32)
    return total


class Chain:
    def __init__(self, steps):
        self.steps, self.result, self.done, self.history = steps, None, False, []
        self.advance(None)

    def advance(self, received):
        try:
            self.wanted = self.steps.send(received)
        except StopIteration as end:
            self.wanted, self.result, self.done = [], end.value, True


class Rounds:
    def __init__(self, lag):
        self.lag, self.count, self.chains = lag, 0, []

    def __call__(self, *chains):
        self.chains += [c for c in chains if c not in self.chains]
        for c in chains:
            if c.done:
                continue
            others = [
                v
                for other in self.chains
                if other is not c
                for when, got in other.history
                if when == self.count - self.lag
                for v in got
            ]
            values = [v for v, _ in c.wanted]
            if others:
                values[0], _ = lax.optimization_barrier((values[0], others))
            got = [
                lax.ppermute(v, *where) if isinstance(where, tuple) else swap(v, where)
                for v, (_, where) in zip(values, c.wanted)
            ]
            c.history.append((self.count, got))
            c.advance(got)
        self.count += 1


def moments(wide):
    return jnp.concatenate(
        [jnp.sum(wide, axis=-1, keepdims=True), jnp.sum(wide * wide, axis=-1, keepdims=True)], axis=-1
    )


def both_z(partial):
    return partial + swap(partial, ACROSS_Z)


def normalize(wide, sums, gain):
    average = sums[:, :1] / D
    inverse_scale = lax.rsqrt(sums[:, 1:2] / D - average * average + EPSILON)
    normed = (wide - average) * inverse_scale
    return normed, inverse_scale, (normed * gain).astype(BF)


PLAIN = (((1,), (0,)), ((), ()))


TILE = 512
STEPS = 2048 // TILE
PARAMS = pltpu.CompilerParams(
    dimension_semantics=("arbitrary",), vmem_limit_bytes=32 * 1024 * 1024
)
COST = pl.CostEstimate(flops=1000, bytes_accessed=1000, transcendentals=0)


def full(shape):
    return pl.BlockSpec(shape, lambda k: (0,) * len(shape))


def weight_specs(tile, axis):
    where = [lambda k: jnp.minimum(k, STEPS - 1), lambda k: jnp.maximum(k - STEPS, 0)]
    return [
        pl.BlockSpec(tile, (lambda k, w=w: (w(k), 0)) if axis == 0 else (lambda k, w=w: (0, w(k))))
        for w in where
    ]


def product_kernel(dims, x_ref, own_ref, other_ref, sum_ref, sent_ref):
    step = pl.program_id(0)

    @pl.when(step == 0)
    def _():
        sum_ref[...] = jnp.zeros_like(sum_ref)

    @pl.when(step < STEPS)
    def _():
        sum_ref[...] += lax.dot_general(x_ref[...], own_ref[...], dims, preferred_element_type=F32)

    @pl.when(step >= STEPS)
    def _():
        sum_ref[...] += lax.dot_general(x_ref[...], other_ref[...], dims, preferred_element_type=F32)

    @pl.when(step == 2 * STEPS - 1)
    def _():
        sent_ref[...] = sum_ref[...].astype(BF)


def product(x, pair, dims):
    m = x.shape[0]
    tile = (TILE, 1024) if dims == PLAIN else (1024, TILE)
    return pl.pallas_call(
        functools.partial(product_kernel, dims),
        grid=(2 * STEPS,),
        in_specs=[pl.BlockSpec((m, TILE), lambda k: (0, k))]
        + weight_specs(tile, 0 if dims == PLAIN else 1),
        out_specs=[full((m, 1024)), full((m, 1024))],
        out_shape=[jax.ShapeDtypeStruct((m, 1024), F32), jax.ShapeDtypeStruct((m, 1024), BF)],
        compiler_params=PARAMS,
        cost_estimate=COST,
    )(x, *pair)


def forward_kernel(part_ref, other_ref, own_down_ref, other_down_ref, near_ref, far_ref, active):
    step = pl.program_id(0)

    @pl.when(step == 0)
    def _():
        active[...] = gelu_value(part_ref[...] + other_ref[...].astype(F32)).astype(BF)

    def write(weights):
        columns = pl.ds(pl.multiple_of(step * TILE, TILE), TILE)
        term = jnp.dot(active[...], weights, preferred_element_type=F32)
        half = term.shape[0] // 2
        near_ref[:, columns] = term[:half]
        far_ref[:, columns] = term[half:].astype(BF)

    @pl.when(step < STEPS)
    def _():
        write(own_down_ref[...])

    @pl.when(step >= STEPS)
    def _():
        write(other_down_ref[...])


def forward_terms(part, other, down):
    m = part.shape[0]
    return pl.pallas_call(
        forward_kernel,
        grid=(2 * STEPS,),
        in_specs=[full((m, 1024)), full((m, 1024))] + weight_specs((1024, TILE), 1),
        out_specs=[full((m // 2, 4096)), full((m // 2, 4096))],
        out_shape=[
            jax.ShapeDtypeStruct((m // 2, 4096), F32),
            jax.ShapeDtypeStruct((m // 2, 4096), BF),
        ],
        scratch_shapes=[pltpu.VMEM((m, 1024), BF)],
        compiler_params=PARAMS,
        cost_estimate=COST,
    )(part, other, *down)


def gradient_kernel(pre_ref, pre_other_ref, up_ref, up_other_ref, gain_ref, own_ref, other_ref, out_ref, grad):
    step = pl.program_id(0)

    @pl.when(step == 0)
    def _():
        preact = pre_ref[...] + pre_other_ref[...].astype(F32)
        upstream = up_ref[...] + up_other_ref[...].astype(F32)
        rounded = (upstream * gelu_slope(preact)).astype(BF)
        grad[...] = rounded
        wide = rounded.astype(F32)
        lane = lax.broadcasted_iota(jnp.int32, (wide.shape[0], 128), 1)
        totals = [jnp.sum(wide * v, axis=1, keepdims=True) for v in (gain_ref[...], preact)]
        sums = jnp.where(lane == 0, totals[0], jnp.where(lane == 1, totals[1], 0.0))
        out_ref[:, 4096:] = sums.astype(out_ref.dtype)

    def write(weights):
        columns = pl.ds(pl.multiple_of(step * TILE, TILE), TILE)
        term = lax.dot_general(grad[...], weights, CONTRACT, preferred_element_type=F32)
        out_ref[:, columns] = term.astype(out_ref.dtype)

    @pl.when(step < STEPS)
    def _():
        write(own_ref[...])

    @pl.when(step >= STEPS)
    def _():
        write(other_ref[...])


def gradient_term(pre, pre_other, upstream, upstream_other, gain_sums, up, dtype):
    m = pre.shape[0]
    return pl.pallas_call(
        gradient_kernel,
        grid=(2 * STEPS,),
        in_specs=[full((m, 1024))] * 4 + [full((1, 1024))] + weight_specs((TILE, 1024), 0),
        out_specs=full((m, 4224)),
        out_shape=jax.ShapeDtypeStruct((m, 4224), dtype),
        scratch_shapes=[pltpu.VMEM((m, 1024), BF)],
        compiler_params=PARAMS,
        cost_estimate=COST,
    )(pre, pre_other, upstream, upstream_other, gain_sums, *up)


def quick_product(x, pair, dims):
    half = x.shape[1] // 2
    part = lax.dot_general(x[:, :half], pair[0], dims, preferred_element_type=F32) + lax.dot_general(
        x[:, half:], pair[1], dims, preferred_element_type=F32
    )
    return part, part.astype(BF)


def tick(backward_block, forward_rows, products, stored, beside, gain_chain, up, down):
    block = jnp.concatenate([backward_block, forward_rows[None]], axis=0)
    gathered = Chain(gathering(block, (*Z_STEPS, Y_STEPS[0])))
    together = Rounds(1)
    while not gathered.done:
        together(gathered, *beside)
    near, forward_near = gathered.result[:-1], gathered.result[-1]
    gain_sums = gain_chain.result
    forward_far = swap(forward_near, Y_STEPS[1])
    far = swap(near, Y_STEPS[1])

    first = products(after(near, forward_far))
    first_other = swap(rows(*[sent for _, sent in (*first, *stored)]), ACROSS_Z)
    forward_part, sent = product(rows(forward_near, forward_far), up, PLAIN)
    forward_other = swap(sent, ACROSS_Z)
    far = after(far, forward_part, *[part for part, _ in first])
    for chain in beside:
        chain.wanted = [(after(value, forward_far), where) for value, where in chain.wanted]
        together(chain)

    second = products(far)
    second_other = swap(rows(*[sent for _, sent in second]), ACROSS_Z)
    forward_near, sent = forward_terms(forward_part, forward_other, down)
    forward_other = swap(sent, Y_STEPS[1])

    parts = [part for part, _ in first]
    received = first_other.reshape(-1, 64, 1024)
    if stored:
        kept = jnp.concatenate([part for part, _ in stored], axis=0).reshape(-1, 64, 1024)
        near_sums = (kept[0], received[1], parts[0], received[0])
    else:
        near_sums = (parts[0], received[0], parts[1], received[1])
    near_term = gradient_term(*near_sums, gain_sums, up, F32)
    second_other = after(second_other, forward_near, near_term, *[c.result for c in beside[:1]]).reshape(-1, 64, 1024)
    if stored:
        far_sums = (kept[1], received[2], second[0][0], second_other[0])
    else:
        far_sums = (second[0][0], second_other[0], second[1][0], second_other[1])
    far_term = gradient_term(*far_sums, gain_sums, up, BF)

    ending = Chain(scattering(near_term, far_term, forward_near + forward_other.astype(F32)))
    together = Rounds(1)
    while not ending.done:
        together(ending)
    return ending.result[0], ending.result[1]


def summed_over_features(part):
    for pairs in (ACROSS_CORE, ACROSS_Z):
        (other,) = yield [(part, pairs)]
        part = part + other
    return part


def gradient(summed, grad, normed, inverse_scale, gain):
    grad_normed = summed[:, :4096] * gain
    sums = summed[:, 4096:4098] / D
    result = grad.astype(F32) + inverse_scale * (grad_normed - sums[:, :1] - normed * sums[:, 1:2])
    return result.astype(BF)


def passed_along(value, by):
    pairs = [(i, i + by) for i in range(4) if 0 <= i + by < 4]
    return lax.ppermute(value, "section", pairs)


def shards(
    first_inputs, new_batch, stashed, first_grads, new_grads, gains, up_weights, down_weights
):
    core = lax.axis_index("dp") % 2
    section = lax.axis_index("section")

    def all_features(value):
        other = swap(value, ACROSS_CORE)
        kept = [lax.dynamic_slice_in_dim(v, core * 8, 8, axis=0) for v in (value, other)]
        return jnp.concatenate(kept, axis=1)

    first_stash, first_grad, first_in, second_stash, fresh_in, fresh_grad = [
        all_features(v) for v in (stashed[0, 0], first_grads[0], first_inputs[0], stashed[1, 0], new_batch, new_grads)
    ]
    gain = jnp.concatenate([gains, swap(gains, ACROSS_CORE)], axis=1)
    ready = [first_stash, first_grad, first_in, second_stash]

    def both_features(weights):
        other = swap(after(weights, ready), ACROSS_CORE)
        return weights, lax.optimization_barrier(jnp.where(core < 2, other, 0))

    up, down = both_features(up_weights[0]), both_features(down_weights[0])

    gain_high = gains.astype(BF)
    gain_parts = rows(gain_high, (gains - gain_high.astype(F32)).astype(BF), jnp.zeros((14, 2048), BF))
    gain_part = jnp.sum(
        jnp.dot(gain_parts, up_weights[0], preferred_element_type=F32), axis=0, keepdims=True
    )

    wides = [x.astype(F32) for x in (first_in, first_stash, second_stash)]
    sums = both_z(jnp.concatenate([moments(w) for w in wides], axis=-1))
    sums, gain_part = lax.optimization_barrier((sums, gain_part))
    _, _, forward_rows = normalize(wides[0], sums[:, 0:2], gain)
    normed, inverse_scale, backward_rows = normalize(wides[1], sums[:, 2:4], gain)
    normed_2, inverse_scale_2, backward_rows_2 = normalize(wides[2], sums[:, 4:6], gain)

    gathered = Chain(gathering(backward_rows_2[None], (*Y_STEPS, *Z_STEPS)))
    gain_chain = Chain(summed_over_features(gain_part))
    forward_sum, grad_hidden = tick(
        jnp.stack([backward_rows, first_grad]),
        forward_rows,
        lambda block: (quick_product(block[0], up, PLAIN), quick_product(block[1], down, CONTRACT)),
        (),
        [gathered, gain_chain],
        gain_chain,
        up,
        down,
    )
    early_out = (wides[0] + forward_sum[:, :4096]).astype(BF)
    early_grad = gradient(grad_hidden, first_grad, normed, inverse_scale, gain)
    stored_rows = gathered.result.reshape(4, 4, 8, 4096).swapaxes(0, 1).reshape(128, 4096)
    stored = (product(stored_rows, up, PLAIN),)

    passed_out, passed_grad = lax.optimization_barrier((early_out, early_grad))
    passed_out, passed_grad = passed_along(passed_out, 1), passed_along(passed_grad, -1)
    passed_out = after(passed_out, passed_grad)
    later_input = jnp.where(section == 0, fresh_in, passed_out)
    later_incoming = jnp.where(section == 3, fresh_grad, passed_grad)
    wide = later_input.astype(F32)
    _, _, forward_rows_2 = normalize(wide, both_z(moments(wide)), gain)
    forward_sum, grad_hidden = tick(
        later_incoming[None],
        forward_rows_2,
        lambda block: (quick_product(block[0], down, CONTRACT),),
        stored,
        [],
        gain_chain,
        up,
        down,
    )
    later_out = (wide + forward_sum[:, :4096]).astype(BF)
    later_grad = gradient(grad_hidden, later_incoming, normed_2, inverse_scale_2, gain)

    def returned(early, later):
        both = jnp.stack([early, later])
        here = both[:, :, :2048]
        there = swap(both[:, :, 2048:], ACROSS_CORE)
        low = jnp.where(core == 0, here, there)
        high = jnp.where(core == 0, there, here)
        return jnp.concatenate([low, high], axis=1)[:, None]

    return returned(early_out, later_out), returned(early_grad, later_grad)


def solution(mesh):
    return jax.shard_map(
        shards,
        mesh=mesh,
        in_specs=(
            P("section", "tensor", "dp"),
            P("tensor", "dp"),
            P(None, "section", "tensor", "dp"),
            P("section", "tensor", "dp"),
            P("tensor", "dp"),
            P("section", "dp"),
            P("section", "dp", "tensor"),
            P("section", "tensor", "dp"),
        ),
        out_specs=(P(None, "section", "tensor", "dp"), P(None, "section", "tensor", "dp")),
        check_vma=False,
    )
```

```python
import functools

import jax
import jax.numpy as jnp
from jax import lax
from jax.experimental import pallas as pl
from jax.experimental.pallas import tpu as pltpu
from jax.sharding import PartitionSpec as P

D = 8192
EPSILON = 1e-05
SLOPE = 0.7978845608028654
CUBIC = 0.044715
CONTRACT = (((1,), (1,)), ((), ()))
BF = jnp.bfloat16
F32 = jnp.float32

PLANE = ("tensor", "dp")


def place(z_hi, y, z_lo, core):
    return ((z_hi * 4 + y) * 2 + z_lo) * 2 + core


def partner(i, k):
    return i ^ 1 if k == 0 else ((i + 1) % 4 if i % 2 else (i - 1) % 4)


def plane_pairs(rule):
    return [
        (place(z, y, w, c), place(*rule(z, y, w, c)))
        for z in range(4)
        for y in range(4)
        for w in range(2)
        for c in range(2)
    ]


Y_STEPS = [plane_pairs(lambda z, y, w, c, k=k: (z, partner(y, (k + c) % 2), w, c)) for k in range(2)]
Z_STEPS = [plane_pairs(lambda z, y, w, c, k=k: (partner(z, (k + c) % 2), y, w, c)) for k in range(2)]
ACROSS_Z = plane_pairs(lambda z, y, w, c: (z, y, 1 - w, c))
ACROSS_CORE = plane_pairs(lambda z, y, w, c: (z, y, w, 1 - c))


def swap(value, pairs):
    return lax.ppermute(value, PLANE, pairs)


def gelu_value(preact):
    return 0.5 * preact * (1.0 + jnp.tanh(SLOPE * (preact + CUBIC * preact * preact * preact)))


def gelu_slope(preact):
    tangent = jnp.tanh(SLOPE * (preact + CUBIC * preact * preact * preact))
    return 0.5 * (1.0 + tangent) + 0.5 * preact * (1.0 - tangent * tangent) * SLOPE * (
        1.0 + 3.0 * CUBIC * preact * preact
    )


def rows(*parts):
    return jnp.concatenate(parts, axis=0)


def after(value, *others):
    return lax.optimization_barrier((value, others))[0]


def gathering(block, steps):
    for pairs in steps:
        (other,) = yield [(block, pairs)]
        block = jnp.concatenate([block, other], axis=1)
    return block


def scattering(near, far, other_total):
    (other,) = yield [(far.astype(BF), Y_STEPS[1])]
    total = near + other.astype(F32)
    total = jnp.stack([jnp.pad(other_total, ((0, 0), (0, total.shape[1] - other_total.shape[1]))), total])
    for pairs in (Y_STEPS[0], Z_STEPS[1], Z_STEPS[0]):
        half = total.shape[1] // 2
        (other,) = yield [(total[:, half:].astype(BF), pairs)]
        total = total[:, :half] + other.astype(F32)
    return total


class Chain:
    def __init__(self, steps):
        self.steps, self.result, self.done, self.history = steps, None, False, []
        self.advance(None)

    def advance(self, received):
        try:
            self.wanted = self.steps.send(received)
        except StopIteration as end:
            self.wanted, self.result, self.done = [], end.value, True


class Rounds:
    def __init__(self, lag):
        self.lag, self.count, self.chains = lag, 0, []

    def __call__(self, *chains):
        self.chains += [c for c in chains if c not in self.chains]
        for c in chains:
            if c.done:
                continue
            others = [
                v
                for other in self.chains
                if other is not c
                for when, got in other.history
                if when == self.count - self.lag
                for v in got
            ]
            values = [v for v, _ in c.wanted]
            if others:
                values[0], _ = lax.optimization_barrier((values[0], others))
            got = [
                lax.ppermute(v, *where) if isinstance(where, tuple) else swap(v, where)
                for v, (_, where) in zip(values, c.wanted)
            ]
            c.history.append((self.count, got))
            c.advance(got)
        self.count += 1


def moments(wide):
    return jnp.concatenate(
        [jnp.sum(wide, axis=-1, keepdims=True), jnp.sum(wide * wide, axis=-1, keepdims=True)], axis=-1
    )


def both_z(partial):
    return partial + swap(partial, ACROSS_Z)


def normalize(wide, sums, gain):
    average = sums[:, :1] / D
    inverse_scale = lax.rsqrt(sums[:, 1:2] / D - average * average + EPSILON)
    normed = (wide - average) * inverse_scale
    return normed, inverse_scale, (normed * gain).astype(BF)


PLAIN = (((1,), (0,)), ((), ()))


PARAMS = pltpu.CompilerParams(vmem_limit_bytes=32 * 1024 * 1024)
COST = pl.CostEstimate(flops=1000, bytes_accessed=1000, transcendentals=0)
WHOLE = pl.BlockSpec(memory_space=pltpu.VMEM)


def kernel_call(body, n_in, *outs):
    return pl.pallas_call(
        body,
        in_specs=[WHOLE] * n_in,
        out_specs=[WHOLE] * len(outs),
        out_shape=[jax.ShapeDtypeStruct(*o) for o in outs],
        compiler_params=PARAMS,
        cost_estimate=COST,
    )


def product_kernel(dims, x_ref, own_ref, other_ref, sum_ref, sent_ref):
    for n in range(0, 1024, 256):
        columns = slice(n, n + 256)
        own, other = [
            ref[:, columns] if dims == PLAIN else ref[columns, :] for ref in (own_ref, other_ref)
        ]
        total = lax.dot_general(x_ref[:, :2048], own, dims, preferred_element_type=F32)
        total += lax.dot_general(x_ref[:, 2048:], other, dims, preferred_element_type=F32)
        sum_ref[:, columns] = total
        sent_ref[:, columns] = total.astype(BF)


def product(x, pair, dims):
    shape = (x.shape[0], 1024)
    return kernel_call(functools.partial(product_kernel, dims), 3, (shape, F32), (shape, BF))(x, *pair)


def forward_kernel(part_ref, other_ref, own_down_ref, other_down_ref, near_ref, far_ref):
    active = gelu_value(part_ref[...] + other_ref[...].astype(F32)).astype(BF)
    half = active.shape[0] // 2
    for at, ref in ((0, own_down_ref), (2048, other_down_ref)):
        for n in range(0, 2048, 512):
            term = jnp.dot(active, ref[:, n : n + 512], preferred_element_type=F32)
            near_ref[:, at + n : at + n + 512] = term[:half]
            far_ref[:, at + n : at + n + 512] = term[half:].astype(BF)


def forward_terms(part, other, down):
    shape = (part.shape[0] // 2, 4096)
    return kernel_call(forward_kernel, 4, (shape, F32), (shape, BF))(part, other, *down)


def gradient_kernel(pre_ref, pre_other_ref, up_ref, up_other_ref, gain_ref, own_ref, other_ref, out_ref):
    preact = pre_ref[...] + pre_other_ref[...].astype(F32)
    upstream = up_ref[...] + up_other_ref[...].astype(F32)
    rounded = (upstream * gelu_slope(preact)).astype(BF)
    for at, ref in ((0, own_ref), (2048, other_ref)):
        for n in range(0, 2048, 512):
            term = lax.dot_general(rounded, ref[n : n + 512, :], CONTRACT, preferred_element_type=F32)
            out_ref[:, at + n : at + n + 512] = term.astype(out_ref.dtype)
    wide = rounded.astype(F32)
    lane = lax.broadcasted_iota(jnp.int32, (wide.shape[0], 128), 1)
    totals = [jnp.sum(wide * v, axis=1, keepdims=True) for v in (gain_ref[...], preact)]
    sums = jnp.where(lane == 0, totals[0], jnp.where(lane == 1, totals[1], 0.0))
    out_ref[:, 4096:] = sums.astype(out_ref.dtype)


def gradient_term(pre, pre_other, upstream, upstream_other, gain_sums, up, dtype):
    out = ((pre.shape[0], 4224), dtype)
    return kernel_call(gradient_kernel, 7, out)(pre, pre_other, upstream, upstream_other, gain_sums, *up)[0]


def quick_product(x, pair, dims):
    half = x.shape[1] // 2
    part = lax.dot_general(x[:, :half], pair[0], dims, preferred_element_type=F32) + lax.dot_general(
        x[:, half:], pair[1], dims, preferred_element_type=F32
    )
    return part, part.astype(BF)


def tick(backward_block, forward_rows, products, stored, early, late, up, down):
    block = jnp.concatenate([backward_block, forward_rows[None]], axis=0)
    gathered = Chain(gathering(block, (*Z_STEPS, Y_STEPS[0])))
    together = Rounds(1)
    together(gathered)
    gain_chain = early(gathered.wanted[0][0])
    while not gathered.done:
        together(gathered, gain_chain)
    block = gathered.result
    if stored:
        stored_part, stored_sent = stored
        stored_other = swap(stored_sent, ACROSS_Z)
        block = after(block, stored_other)
    near, forward_near = block[:-1], block[-1]
    gain_sums = gain_chain.result
    forward_far = swap(forward_near, Y_STEPS[1])
    far = swap(near, Y_STEPS[1])

    first = products(near, product)
    first_other = swap(rows(*[sent for _, sent in first]), ACROSS_Z).reshape(-1, 64, 1024)
    forward_far = after(forward_far, *[sent for _, sent in first])
    forward_part, sent = product(rows(forward_near, forward_far), up, PLAIN)
    forward_other = swap(sent, ACROSS_Z)
    if stored:
        kept, kept_other = stored_part.reshape(2, 64, 1024), stored_other.reshape(2, 64, 1024)
        near_sums = (kept[0], kept_other[0], first[0][0], first_other[0])
    else:
        near_sums = (first[0][0], first_other[0], first[1][0], first_other[1])
    near_term = gradient_term(*near_sums, gain_sums, up, F32)
    far = after(far, forward_part, near_term)

    second = products(far, quick_product)
    second_other = swap(rows(*[sent for _, sent in second]), ACROSS_Z)
    forward_near, sent = forward_terms(forward_part, forward_other, down)
    forward_other = swap(sent, Y_STEPS[1])
    second_other = after(second_other, forward_near).reshape(-1, 64, 1024)
    if stored:
        far_sums = (kept[1], kept_other[1], second[0][0], second_other[0])
    else:
        far_sums = (second[0][0], second_other[0], second[1][0], second_other[1])
    far_term = gradient_term(*far_sums, gain_sums, up, BF)

    ending = Chain(scattering(near_term, far_term, forward_near + forward_other.astype(F32)))
    together = Rounds(1)
    while not ending.done:
        together(ending, *late)
    return ending.result[0], ending.result[1]


def summed_over_features(part):
    for pairs in (ACROSS_CORE, ACROSS_Z):
        (other,) = yield [(part, pairs)]
        part = part + other
    return part


def gradient(summed, grad, normed, inverse_scale, gain):
    grad_normed = summed[:, :4096] * gain
    sums = summed[:, 4096:4098] / D
    result = grad.astype(F32) + inverse_scale * (grad_normed - sums[:, :1] - normed * sums[:, 1:2])
    return result.astype(BF)


def passed_along(value, by):
    pairs = [(i, i + by) for i in range(4) if 0 <= i + by < 4]
    return lax.ppermute(value, "section", pairs)


def shards(
    first_inputs, new_batch, stashed, first_grads, new_grads, gains, up_weights, down_weights
):
    core = lax.axis_index("dp") % 2
    section = lax.axis_index("section")

    def all_features(value):
        other = swap(value, ACROSS_CORE)
        kept = [lax.dynamic_slice_in_dim(v, core * 8, 8, axis=0) for v in (value, other)]
        return jnp.concatenate(kept, axis=1)

    first_stash, first_grad, first_in = [
        all_features(v) for v in (stashed[0, 0], first_grads[0], first_inputs[0])
    ]
    gain = jnp.concatenate([gains, swap(gains, ACROSS_CORE)], axis=1)
    ready = [first_stash, first_grad, first_in]

    def both_features(weights):
        other = swap(after(weights, ready), ACROSS_CORE)
        return weights, lax.optimization_barrier(jnp.where(core < 2, other, 0))

    up, down = both_features(up_weights[0]), both_features(down_weights[0])

    gain_high = gains.astype(BF)
    gain_parts = rows(gain_high, (gains - gain_high.astype(F32)).astype(BF), jnp.zeros((14, 2048), BF))
    gain_parts = jnp.pad(gain_parts, ((0, 0), (0, 2048)))
    gain_chains = []

    def early(block):
        part = product(after(gain_parts, block), (up_weights[0], up_weights[0]), PLAIN)[0]
        gain_chains.append(Chain(summed_over_features(jnp.sum(part, axis=0, keepdims=True))))
        return gain_chains[0]

    wides = [x.astype(F32) for x in (first_in, first_stash)]
    sums = both_z(jnp.concatenate([moments(w) for w in wides], axis=-1))
    _, _, forward_rows = normalize(wides[0], sums[:, 0:2], gain)
    normed, inverse_scale, backward_rows = normalize(wides[1], sums[:, 2:4], gain)

    later = lax.optimization_barrier(((stashed[1, 0], new_batch, new_grads), forward_rows))[0]
    second_stash, fresh_in, fresh_grad = [all_features(v) for v in later]
    wide = second_stash.astype(F32)
    normed_2, inverse_scale_2, backward_rows_2 = normalize(wide, both_z(moments(wide)), gain)

    gathered = Chain(gathering(backward_rows_2[None], (*Z_STEPS, *Y_STEPS)))
    forward_sum, grad_hidden = tick(
        jnp.stack([backward_rows, first_grad]),
        forward_rows,
        lambda block, multiply: (multiply(block[0], up, PLAIN), multiply(block[1], down, CONTRACT)),
        (),
        early,
        [gathered],
        up,
        down,
    )
    early_out = (wides[0] + forward_sum[:, :4096]).astype(BF)
    early_grad = gradient(grad_hidden, first_grad, normed, inverse_scale, gain)
    stored_part, stored_sent = product(gathered.result[0], up, PLAIN)

    passed_out, passed_grad = lax.optimization_barrier((early_out, early_grad))
    passed_out, passed_grad = passed_along(passed_out, 1), passed_along(passed_grad, -1)
    passed_out = after(passed_out, passed_grad)
    later_input = jnp.where(section == 0, fresh_in, passed_out)
    later_incoming = jnp.where(section == 3, fresh_grad, passed_grad)
    wide = later_input.astype(F32)
    _, _, forward_rows_2 = normalize(wide, after(both_z(moments(wide)), gathered.result), gain)
    forward_sum, grad_hidden = tick(
        later_incoming[None],
        forward_rows_2,
        lambda block, multiply: (multiply(block[0], down, CONTRACT),),
        (stored_part, stored_sent),
        lambda block: gain_chains[0],
        [],
        up,
        down,
    )
    later_out = (wide + forward_sum[:, :4096]).astype(BF)
    later_grad = gradient(grad_hidden, later_incoming, normed_2, inverse_scale_2, gain)

    def returned(early, later):
        both = jnp.stack([early, later])
        here = both[:, :, :2048]
        there = swap(both[:, :, 2048:], ACROSS_CORE)
        low = jnp.where(core == 0, here, there)
        high = jnp.where(core == 0, there, here)
        return jnp.concatenate([low, high], axis=1)[:, None]

    return returned(early_out, later_out), returned(early_grad, later_grad)


def solution(mesh):
    return jax.shard_map(
        shards,
        mesh=mesh,
        in_specs=(
            P("section", "tensor", "dp"),
            P("tensor", "dp"),
            P(None, "section", "tensor", "dp"),
            P("section", "tensor", "dp"),
            P("tensor", "dp"),
            P("section", "dp"),
            P("section", "dp", "tensor"),
            P("section", "tensor", "dp"),
        ),
        out_specs=(P(None, "section", "tensor", "dp"), P(None, "section", "tensor", "dp")),
        check_vma=False,
    )
```

```python
import functools

import jax
import jax.numpy as jnp
from jax import lax
from jax.experimental import pallas as pl
from jax.experimental.pallas import tpu as pltpu
from jax.sharding import PartitionSpec as P

D = 8192
EPSILON = 1e-05
SLOPE = 0.7978845608028654
CUBIC = 0.044715
CONTRACT = (((1,), (1,)), ((), ()))
BF = jnp.bfloat16
F32 = jnp.float32

PLANE = ("tensor", "dp")


def place(z_hi, y, z_lo, core):
    return ((z_hi * 4 + y) * 2 + z_lo) * 2 + core


def partner(i, k):
    return i ^ 1 if k == 0 else ((i + 1) % 4 if i % 2 else (i - 1) % 4)


def plane_pairs(rule):
    return [
        (place(z, y, w, c), place(*rule(z, y, w, c)))
        for z in range(4)
        for y in range(4)
        for w in range(2)
        for c in range(2)
    ]


Y_STEPS = [plane_pairs(lambda z, y, w, c, k=k: (z, partner(y, (k + c) % 2), w, c)) for k in range(2)]
Z_STEPS = [plane_pairs(lambda z, y, w, c, k=k: (partner(z, (k + c) % 2), y, w, c)) for k in range(2)]
ACROSS_Z = plane_pairs(lambda z, y, w, c: (z, y, 1 - w, c))
ACROSS_CORE = plane_pairs(lambda z, y, w, c: (z, y, w, 1 - c))


def swap(value, pairs):
    return lax.ppermute(value, PLANE, pairs)


def gelu_value(preact):
    return 0.5 * preact * (1.0 + jnp.tanh(SLOPE * (preact + CUBIC * preact * preact * preact)))


def gelu_slope(preact):
    tangent = jnp.tanh(SLOPE * (preact + CUBIC * preact * preact * preact))
    return 0.5 * (1.0 + tangent) + 0.5 * preact * (1.0 - tangent * tangent) * SLOPE * (
        1.0 + 3.0 * CUBIC * preact * preact
    )


def rows(*parts):
    return jnp.concatenate(parts, axis=0)


def after(value, *others):
    return lax.optimization_barrier((value, others))[0]


def gathering(block, steps):
    for pairs in steps:
        (other,) = yield [(block, pairs)]
        block = jnp.concatenate([block, other], axis=1)
    return block


def scattering(near, far, other_total):
    (other,) = yield [(far.astype(BF), Y_STEPS[1])]
    total = near + other.astype(F32)
    total = jnp.stack([jnp.pad(other_total, ((0, 0), (0, total.shape[1] - other_total.shape[1]))), total])
    for pairs in (Y_STEPS[0], Z_STEPS[1], Z_STEPS[0]):
        half = total.shape[1] // 2
        (other,) = yield [(total[:, half:].astype(BF), pairs)]
        total = total[:, :half] + other.astype(F32)
    return total


class Chain:
    def __init__(self, steps):
        self.steps, self.result, self.done, self.history = steps, None, False, []
        self.advance(None)

    def advance(self, received):
        try:
            self.wanted = self.steps.send(received)
        except StopIteration as end:
            self.wanted, self.result, self.done = [], end.value, True


class Rounds:
    def __init__(self, lag):
        self.lag, self.count, self.chains = lag, 0, []

    def __call__(self, *chains):
        self.chains += [c for c in chains if c not in self.chains]
        for c in chains:
            if c.done:
                continue
            others = [
                v
                for other in self.chains
                if other is not c
                for when, got in other.history
                if when == self.count - self.lag
                for v in got
            ]
            values = [v for v, _ in c.wanted]
            if others:
                values[0], _ = lax.optimization_barrier((values[0], others))
            got = [
                lax.ppermute(v, *where) if isinstance(where, tuple) else swap(v, where)
                for v, (_, where) in zip(values, c.wanted)
            ]
            c.history.append((self.count, got))
            c.advance(got)
        self.count += 1


def moments(wide):
    return jnp.concatenate(
        [jnp.sum(wide, axis=-1, keepdims=True), jnp.sum(wide * wide, axis=-1, keepdims=True)], axis=-1
    )


def both_z(partial):
    return partial + swap(partial, ACROSS_Z)


def normalize(wide, sums, gain):
    average = sums[:, :1] / D
    inverse_scale = lax.rsqrt(sums[:, 1:2] / D - average * average + EPSILON)
    normed = (wide - average) * inverse_scale
    return normed, inverse_scale, (normed * gain).astype(BF)


PLAIN = (((1,), (0,)), ((), ()))


PARAMS = pltpu.CompilerParams(vmem_limit_bytes=32 * 1024 * 1024)
COST = pl.CostEstimate(flops=1000, bytes_accessed=1000, transcendentals=0)
WHOLE = pl.BlockSpec(memory_space=pltpu.VMEM)


def kernel_call(body, n_in, *outs, awaited=()):
    def kernel(*refs):
        body(*refs[:n_in], *refs[n_in + len(awaited) :])

    call = pl.pallas_call(
        kernel,
        in_specs=[WHOLE] * n_in + [pl.BlockSpec(memory_space=pl.ANY)] * len(awaited),
        out_specs=[WHOLE] * len(outs),
        out_shape=[jax.ShapeDtypeStruct(*o) for o in outs],
        compiler_params=PARAMS,
        cost_estimate=COST,
    )
    return lambda *operands: call(*operands, *awaited)


def product_kernel(dims, x_ref, own_ref, other_ref, sum_ref, sent_ref):
    for n in range(0, 1024, 256):
        columns = slice(n, n + 256)
        own, other = [
            ref[:, columns] if dims == PLAIN else ref[columns, :] for ref in (own_ref, other_ref)
        ]
        total = lax.dot_general(x_ref[:, :2048], own, dims, preferred_element_type=F32)
        total += lax.dot_general(x_ref[:, 2048:], other, dims, preferred_element_type=F32)
        sum_ref[:, columns] = total
        sent_ref[:, columns] = total.astype(BF)


def product(x, pair, dims, awaited=()):
    shape = (x.shape[0], 1024)
    call = kernel_call(
        functools.partial(product_kernel, dims), 3, (shape, F32), (shape, BF), awaited=awaited
    )
    return call(x, *pair)


def forward_kernel(part_ref, other_ref, own_down_ref, other_down_ref, near_ref, far_ref):
    active = gelu_value(part_ref[...] + other_ref[...].astype(F32)).astype(BF)
    half = active.shape[0] // 2
    for at, ref in ((0, own_down_ref), (2048, other_down_ref)):
        for n in range(0, 2048, 512):
            term = jnp.dot(active, ref[:, n : n + 512], preferred_element_type=F32)
            near_ref[:, at + n : at + n + 512] = term[:half]
            far_ref[:, at + n : at + n + 512] = term[half:].astype(BF)


def forward_terms(part, other, down, awaited):
    shape = (part.shape[0] // 2, 4096)
    call = kernel_call(forward_kernel, 4, (shape, F32), (shape, BF), awaited=awaited)
    return call(part, other, *down)


def gradient_kernel(pre_ref, pre_other_ref, up_ref, up_other_ref, gain_ref, own_ref, other_ref, out_ref):
    preact = pre_ref[...] + pre_other_ref[...].astype(F32)
    upstream = up_ref[...] + up_other_ref[...].astype(F32)
    rounded = (upstream * gelu_slope(preact)).astype(BF)
    for at, ref in ((0, own_ref), (2048, other_ref)):
        for n in range(0, 2048, 512):
            term = lax.dot_general(rounded, ref[n : n + 512, :], CONTRACT, preferred_element_type=F32)
            out_ref[:, at + n : at + n + 512] = term.astype(out_ref.dtype)
    wide = rounded.astype(F32)
    lane = lax.broadcasted_iota(jnp.int32, (wide.shape[0], 128), 1)
    totals = [jnp.sum(wide * v, axis=1, keepdims=True) for v in (gain_ref[...], preact)]
    sums = jnp.where(lane == 0, totals[0], jnp.where(lane == 1, totals[1], 0.0))
    out_ref[:, 4096:] = sums.astype(out_ref.dtype)


def gradient_term(pre, pre_other, upstream, upstream_other, gain_sums, up, dtype):
    out = ((pre.shape[0], 4224), dtype)
    return kernel_call(gradient_kernel, 7, out)(pre, pre_other, upstream, upstream_other, gain_sums, *up)[0]


def quick_product(x, pair, dims):
    half = x.shape[1] // 2
    part = lax.dot_general(x[:, :half], pair[0], dims, preferred_element_type=F32) + lax.dot_general(
        x[:, half:], pair[1], dims, preferred_element_type=F32
    )
    return part, part.astype(BF)


def tick(backward_block, forward_rows, products, stored, early, late, up, down):
    block = jnp.concatenate([backward_block, forward_rows[None]], axis=0)
    gathered = Chain(gathering(block, (*Z_STEPS, Y_STEPS[0])))
    together = Rounds(1)
    together(gathered)
    gain_chain = early(gathered.wanted[0][0])
    while not gathered.done:
        together(gathered, gain_chain)
    block = gathered.result
    if stored:
        stored_part, stored_sent = stored
        stored_other = swap(stored_sent, ACROSS_Z)
        block = after(block, stored_other)
    near, forward_near = block[:-1], block[-1]
    gain_sums = gain_chain.result
    forward_far = swap(forward_near, Y_STEPS[1])
    far = swap(near, Y_STEPS[1])

    first = products(near, product)
    first_other = swap(rows(*[sent for _, sent in first]), ACROSS_Z).reshape(-1, 64, 1024)
    forward_far = after(forward_far, *[sent for _, sent in first])
    awaited = (first_other,) if stored else ()
    forward_part, sent = product(rows(forward_near, forward_far), up, PLAIN, awaited)
    forward_other = swap(sent, ACROSS_Z)
    if stored:
        kept, kept_other = stored_part.reshape(2, 64, 1024), stored_other.reshape(2, 64, 1024)
        near_sums = (kept[0], kept_other[0], first[0][0], first_other[0])
    else:
        near_sums = (first[0][0], first_other[0], first[1][0], first_other[1])
    near_term = gradient_term(*near_sums, gain_sums, up, F32)
    far = after(far, forward_part, near_term)

    second = products(far, quick_product)
    second_other = swap(rows(*[sent for _, sent in second]), ACROSS_Z)
    forward_near, sent = forward_terms(forward_part, forward_other, down, (second[-1][1],))
    forward_other = swap(sent, Y_STEPS[1])
    second_other = after(second_other, forward_near).reshape(-1, 64, 1024)
    if stored:
        far_sums = (kept[1], kept_other[1], second[0][0], second_other[0])
    else:
        far_sums = (second[0][0], second_other[0], second[1][0], second_other[1])
    far_term = gradient_term(*far_sums, gain_sums, up, BF)

    ending = Chain(scattering(near_term, far_term, forward_near + forward_other.astype(F32)))
    together = Rounds(1)
    while not ending.done:
        together(ending, *late)
    return ending.result[0], ending.result[1]


def summed_over_features(part):
    for pairs in (ACROSS_CORE, ACROSS_Z):
        (other,) = yield [(part, pairs)]
        part = part + other
    return part


def gradient(summed, grad, normed, inverse_scale, gain):
    grad_normed = summed[:, :4096] * gain
    sums = summed[:, 4096:4098] / D
    result = grad.astype(F32) + inverse_scale * (grad_normed - sums[:, :1] - normed * sums[:, 1:2])
    return result.astype(BF)


def passed_along(value, by):
    pairs = [(i, i + by) for i in range(4) if 0 <= i + by < 4]
    return lax.ppermute(value, "section", pairs)


def shards(
    first_inputs, new_batch, stashed, first_grads, new_grads, gains, up_weights, down_weights
):
    core = lax.axis_index("dp") % 2
    section = lax.axis_index("section")

    def all_features(value):
        other = swap(value, ACROSS_CORE)
        kept = [lax.dynamic_slice_in_dim(v, core * 8, 8, axis=0) for v in (value, other)]
        return jnp.concatenate(kept, axis=1)

    first_stash, first_grad, first_in = [
        all_features(v) for v in (stashed[0, 0], first_grads[0], first_inputs[0])
    ]
    gain = jnp.concatenate([gains, swap(gains, ACROSS_CORE)], axis=1)
    ready = [first_stash, first_grad, first_in]

    def both_features(weights):
        other = swap(after(weights, ready), ACROSS_CORE)
        return weights, lax.optimization_barrier(jnp.where(core < 2, other, 0))

    up, down = both_features(up_weights[0]), both_features(down_weights[0])

    gain_high = gains.astype(BF)
    gain_parts = rows(gain_high, (gains - gain_high.astype(F32)).astype(BF), jnp.zeros((14, 2048), BF))
    gain_parts = jnp.pad(gain_parts, ((0, 0), (0, 2048)))
    gain_chains = []

    def early(block):
        part = product(after(gain_parts, block), (up_weights[0], up_weights[0]), PLAIN)[0]
        gain_chains.append(Chain(summed_over_features(jnp.sum(part, axis=0, keepdims=True))))
        return gain_chains[0]

    wides = [x.astype(F32) for x in (first_in, first_stash)]
    sums = both_z(jnp.concatenate([moments(w) for w in wides], axis=-1))
    _, _, forward_rows = normalize(wides[0], sums[:, 0:2], gain)
    normed, inverse_scale, backward_rows = normalize(wides[1], sums[:, 2:4], gain)

    later = lax.optimization_barrier(((stashed[1, 0], new_batch, new_grads), forward_rows))[0]
    second_stash, fresh_in, fresh_grad = [all_features(v) for v in later]
    wide = second_stash.astype(F32)
    normed_2, inverse_scale_2, backward_rows_2 = normalize(wide, both_z(moments(wide)), gain)

    gathered = Chain(gathering(backward_rows_2[None], (*Z_STEPS, *Y_STEPS)))
    forward_sum, grad_hidden = tick(
        jnp.stack([backward_rows, first_grad]),
        forward_rows,
        lambda block, multiply: (multiply(block[0], up, PLAIN), multiply(block[1], down, CONTRACT)),
        (),
        early,
        [gathered],
        up,
        down,
    )
    early_out = (wides[0] + forward_sum[:, :4096]).astype(BF)
    early_grad = gradient(grad_hidden, first_grad, normed, inverse_scale, gain)
    stored_part, stored_sent = product(gathered.result[0], up, PLAIN)

    passed_out, passed_grad = lax.optimization_barrier((early_out, early_grad))
    passed_out, passed_grad = passed_along(passed_out, 1), passed_along(passed_grad, -1)
    passed_out = after(passed_out, passed_grad)
    later_input = jnp.where(section == 0, fresh_in, passed_out)
    later_incoming = jnp.where(section == 3, fresh_grad, passed_grad)
    wide = later_input.astype(F32)
    _, _, forward_rows_2 = normalize(wide, after(both_z(moments(wide)), gathered.result), gain)
    forward_sum, grad_hidden = tick(
        later_incoming[None],
        forward_rows_2,
        lambda block, multiply: (multiply(block[0], down, CONTRACT),),
        (stored_part, stored_sent),
        lambda block: gain_chains[0],
        [],
        up,
        down,
    )
    later_out = (wide + forward_sum[:, :4096]).astype(BF)
    later_grad = gradient(grad_hidden, later_incoming, normed_2, inverse_scale_2, gain)

    def returned(early, later):
        both = jnp.stack([early, later])
        here = both[:, :, :2048]
        there = swap(both[:, :, 2048:], ACROSS_CORE)
        low = jnp.where(core == 0, here, there)
        high = jnp.where(core == 0, there, here)
        return jnp.concatenate([low, high], axis=1)[:, None]

    return returned(early_out, later_out), returned(early_grad, later_grad)


def solution(mesh):
    return jax.shard_map(
        shards,
        mesh=mesh,
        in_specs=(
            P("section", "tensor", "dp"),
            P("tensor", "dp"),
            P(None, "section", "tensor", "dp"),
            P("section", "tensor", "dp"),
            P("tensor", "dp"),
            P("section", "dp"),
            P("section", "dp", "tensor"),
            P("section", "tensor", "dp"),
        ),
        out_specs=(P(None, "section", "tensor", "dp"), P(None, "section", "tensor", "dp")),
        check_vma=False,
    )
```

```python
import functools

import jax
import jax.numpy as jnp
from jax import lax
from jax.experimental import pallas as pl
from jax.experimental.pallas import tpu as pltpu
from jax.sharding import PartitionSpec as P

D = 8192
EPSILON = 1e-05
SLOPE = 0.7978845608028654
CUBIC = 0.044715
CONTRACT = (((1,), (1,)), ((), ()))
BF = jnp.bfloat16
F32 = jnp.float32

PLANE = ("tensor", "dp")


def place(z_hi, y, z_lo, core):
    return ((z_hi * 4 + y) * 2 + z_lo) * 2 + core


def partner(i, k):
    return i ^ 1 if k == 0 else ((i + 1) % 4 if i % 2 else (i - 1) % 4)


def plane_pairs(rule):
    return [
        (place(z, y, w, c), place(*rule(z, y, w, c)))
        for z in range(4)
        for y in range(4)
        for w in range(2)
        for c in range(2)
    ]


Y_STEPS = [plane_pairs(lambda z, y, w, c, k=k: (z, partner(y, (k + c) % 2), w, c)) for k in range(2)]
Z_STEPS = [plane_pairs(lambda z, y, w, c, k=k: (partner(z, (k + c) % 2), y, w, c)) for k in range(2)]
ACROSS_Z = plane_pairs(lambda z, y, w, c: (z, y, 1 - w, c))
ACROSS_CORE = plane_pairs(lambda z, y, w, c: (z, y, w, 1 - c))


def swap(value, pairs):
    return lax.ppermute(value, PLANE, pairs)


def gelu_value(preact):
    return 0.5 * preact * (1.0 + jnp.tanh(SLOPE * (preact + CUBIC * preact * preact * preact)))


def gelu_slope(preact):
    tangent = jnp.tanh(SLOPE * (preact + CUBIC * preact * preact * preact))
    return 0.5 * (1.0 + tangent) + 0.5 * preact * (1.0 - tangent * tangent) * SLOPE * (
        1.0 + 3.0 * CUBIC * preact * preact
    )


def rows(*parts):
    return jnp.concatenate(parts, axis=0)


def after(value, *others):
    return lax.optimization_barrier((value, others))[0]


def gathering(block, steps):
    for pairs in steps:
        (other,) = yield [(block, pairs)]
        block = jnp.concatenate([block, other], axis=1)
    return block


def scattering(near, far, other_total):
    (other,) = yield [(far.astype(BF), Y_STEPS[1])]
    total = near + other.astype(F32)
    total = jnp.stack([jnp.pad(other_total, ((0, 0), (0, total.shape[1] - other_total.shape[1]))), total])
    for pairs in (Y_STEPS[0], Z_STEPS[1], Z_STEPS[0]):
        half = total.shape[1] // 2
        (other,) = yield [(total[:, half:].astype(BF), pairs)]
        total = total[:, :half] + other.astype(F32)
    return total


class Chain:
    def __init__(self, steps):
        self.steps, self.result, self.done, self.history = steps, None, False, []
        self.advance(None)

    def advance(self, received):
        try:
            self.wanted = self.steps.send(received)
        except StopIteration as end:
            self.wanted, self.result, self.done = [], end.value, True


class Rounds:
    def __init__(self, lag):
        self.lag, self.count, self.chains = lag, 0, []

    def __call__(self, *chains):
        self.chains += [c for c in chains if c not in self.chains]
        for c in chains:
            if c.done:
                continue
            others = [
                v
                for other in self.chains
                if other is not c
                for when, got in other.history
                if when == self.count - self.lag
                for v in got
            ]
            values = [v for v, _ in c.wanted]
            if others:
                values[0], _ = lax.optimization_barrier((values[0], others))
            got = [
                lax.ppermute(v, *where) if isinstance(where, tuple) else swap(v, where)
                for v, (_, where) in zip(values, c.wanted)
            ]
            c.history.append((self.count, got))
            c.advance(got)
        self.count += 1


def moments(wide):
    return jnp.concatenate(
        [jnp.sum(wide, axis=-1, keepdims=True), jnp.sum(wide * wide, axis=-1, keepdims=True)], axis=-1
    )


def both_z(partial):
    return partial + swap(partial, ACROSS_Z)


def normalize(wide, sums, gain):
    average = sums[:, :1] / D
    inverse_scale = lax.rsqrt(sums[:, 1:2] / D - average * average + EPSILON)
    normed = (wide - average) * inverse_scale
    return normed, inverse_scale, (normed * gain).astype(BF)


PLAIN = (((1,), (0,)), ((), ()))


PARAMS = pltpu.CompilerParams(vmem_limit_bytes=32 * 1024 * 1024)
COST = pl.CostEstimate(flops=1000, bytes_accessed=1000, transcendentals=0)
WHOLE = pl.BlockSpec(memory_space=pltpu.VMEM)


def kernel_call(body, n_in, *outs, awaited=()):
    def kernel(*refs):
        body(*refs[:n_in], *refs[n_in + len(awaited) :])

    call = pl.pallas_call(
        kernel,
        in_specs=[WHOLE] * n_in + [pl.BlockSpec(memory_space=pl.ANY)] * len(awaited),
        out_specs=[WHOLE] * len(outs),
        out_shape=[jax.ShapeDtypeStruct(*o) for o in outs],
        compiler_params=PARAMS,
        cost_estimate=COST,
    )
    return lambda *operands: call(*operands, *awaited)


def copy_kernel(in_ref, out_ref):
    out_ref[...] = in_ref[...]


def product_kernel(dims, x_ref, own_ref, other_ref, sum_ref, sent_ref):
    for n in range(0, 1024, 256):
        columns = slice(n, n + 256)
        own, other = [
            ref[:, columns] if dims == PLAIN else ref[columns, :] for ref in (own_ref, other_ref)
        ]
        total = lax.dot_general(x_ref[:, :2048], own, dims, preferred_element_type=F32)
        total += lax.dot_general(x_ref[:, 2048:], other, dims, preferred_element_type=F32)
        sum_ref[:, columns] = total
        sent_ref[:, columns] = total.astype(BF)


def product(x, pair, dims, awaited=()):
    shape = (x.shape[0], 1024)
    call = kernel_call(
        functools.partial(product_kernel, dims), 3, (shape, F32), (shape, BF), awaited=awaited
    )
    return call(x, *pair)


def forward_kernel(part_ref, other_ref, own_down_ref, other_down_ref, near_ref, far_ref):
    active = gelu_value(part_ref[...] + other_ref[...].astype(F32)).astype(BF)
    half = active.shape[0] // 2
    for at, ref in ((0, own_down_ref), (2048, other_down_ref)):
        for n in range(0, 2048, 512):
            term = jnp.dot(active, ref[:, n : n + 512], preferred_element_type=F32)
            near_ref[:, at + n : at + n + 512] = term[:half]
            far_ref[:, at + n : at + n + 512] = term[half:].astype(BF)


def forward_terms(part, other, down, awaited):
    shape = (part.shape[0] // 2, 4096)
    call = kernel_call(forward_kernel, 4, (shape, F32), (shape, BF), awaited=awaited)
    return call(part, other, *down)


def gradient_kernel(pre_ref, pre_other_ref, up_ref, up_other_ref, gain_ref, own_ref, other_ref, out_ref):
    preact = pre_ref[...] + pre_other_ref[...].astype(F32)
    upstream = up_ref[...] + up_other_ref[...].astype(F32)
    rounded = (upstream * gelu_slope(preact)).astype(BF)
    for at, ref in ((0, own_ref), (2048, other_ref)):
        for n in range(0, 2048, 512):
            term = lax.dot_general(rounded, ref[n : n + 512, :], CONTRACT, preferred_element_type=F32)
            out_ref[:, at + n : at + n + 512] = term.astype(out_ref.dtype)
    wide = rounded.astype(F32)
    lane = lax.broadcasted_iota(jnp.int32, (wide.shape[0], 128), 1)
    totals = [jnp.sum(wide * v, axis=1, keepdims=True) for v in (gain_ref[...], preact)]
    sums = jnp.where(lane == 0, totals[0], jnp.where(lane == 1, totals[1], 0.0))
    out_ref[:, 4096:] = sums.astype(out_ref.dtype)


def gradient_term(pre, pre_other, upstream, upstream_other, gain_sums, up, dtype):
    out = ((pre.shape[0], 4224), dtype)
    return kernel_call(gradient_kernel, 7, out)(pre, pre_other, upstream, upstream_other, gain_sums, *up)[0]


def quick_product(x, pair, dims):
    half = x.shape[1] // 2
    part = lax.dot_general(x[:, :half], pair[0], dims, preferred_element_type=F32) + lax.dot_general(
        x[:, half:], pair[1], dims, preferred_element_type=F32
    )
    return part, part.astype(BF)


def tick(backward_block, forward_rows, products, stored, early, late, up, down):
    block = jnp.concatenate([backward_block, forward_rows[None]], axis=0)
    gathered = Chain(gathering(block, (*Z_STEPS, Y_STEPS[0])))
    together = Rounds(1)
    together(gathered)
    gain_chain = early(gathered.wanted[0][0])
    while not gathered.done:
        together(gathered, gain_chain)
    block = gathered.result
    if stored:
        stored_part, stored_sent = stored
        stored_other = swap(stored_sent, ACROSS_Z)
        block = after(block, stored_other)
    near, forward_near = block[:-1], block[-1]
    gain_sums = gain_chain.result
    forward_far = swap(forward_near, Y_STEPS[1])
    far = swap(near, Y_STEPS[1])

    first = products(near, product)
    first_other = swap(rows(*[sent for _, sent in first]), ACROSS_Z).reshape(-1, 64, 1024)
    forward_far = after(forward_far, *[sent for _, sent in first])
    awaited = (first_other,) if stored else ()
    forward_part, sent = product(rows(forward_near, forward_far), up, PLAIN, awaited)
    forward_other = swap(sent, ACROSS_Z)
    if stored:
        kept, kept_other = stored_part.reshape(2, 64, 1024), stored_other.reshape(2, 64, 1024)
        near_sums = (kept[0], kept_other[0], first[0][0], first_other[0])
    else:
        near_sums = (first[0][0], first_other[0], first[1][0], first_other[1])
    near_term = gradient_term(*near_sums, gain_sums, up, F32)
    far = after(far, forward_part, near_term)

    second = products(far, quick_product)
    second_other = swap(rows(*[sent for _, sent in second]), ACROSS_Z)
    forward_near, sent = forward_terms(forward_part, forward_other, down, (second[-1][1],))
    forward_other = swap(sent, Y_STEPS[1])
    second_other = after(second_other, forward_near).reshape(-1, 64, 1024)
    if stored:
        far_sums = (kept[1], kept_other[1], second[0][0], second_other[0])
    else:
        far_sums = (second[0][0], second_other[0], second[1][0], second_other[1])
    far_term = gradient_term(*far_sums, gain_sums, up, BF)

    ending = Chain(scattering(near_term, far_term, forward_near + forward_other.astype(F32)))
    together = Rounds(1)
    while not ending.done:
        together(ending, *late)
    return ending.result[0], ending.result[1]


def summed_over_features(part):
    for pairs in (ACROSS_CORE, ACROSS_Z):
        (other,) = yield [(part, pairs)]
        part = part + other
    return part


def gradient(summed, grad, normed, inverse_scale, gain):
    grad_normed = summed[:, :4096] * gain
    sums = summed[:, 4096:4098] / D
    result = grad.astype(F32) + inverse_scale * (grad_normed - sums[:, :1] - normed * sums[:, 1:2])
    return result.astype(BF)


def passed_along(value, by):
    pairs = [(i, i + by) for i in range(4) if 0 <= i + by < 4]
    return lax.ppermute(value, "section", pairs)


def shards(
    first_inputs, new_batch, stashed, first_grads, new_grads, gains, up_weights, down_weights
):
    core = lax.axis_index("dp") % 2
    section = lax.axis_index("section")

    def all_features(value, which):
        other = swap(value, ACROSS_CORE)
        kept = [lax.dynamic_slice_in_dim(v, which * 8, 8, axis=0) for v in (value, other)]
        return jnp.concatenate(kept, axis=1)

    first_stash, first_grad, first_in = [
        all_features(v, core) for v in (stashed[0, 0], first_grads[0], first_inputs[0])
    ]
    gain = jnp.concatenate([gains, swap(gains, ACROSS_CORE)], axis=1)
    ready = [first_stash, first_grad, first_in]

    def both_features(weights):
        other = swap(after(weights, ready), ACROSS_CORE)
        return weights, lax.optimization_barrier(jnp.where(core < 2, other, 0))

    up, down = both_features(up_weights[0]), both_features(down_weights[0])

    gain_high = gains.astype(BF)
    gain_parts = rows(gain_high, (gains - gain_high.astype(F32)).astype(BF), jnp.zeros((14, 2048), BF))
    gain_parts = jnp.pad(gain_parts, ((0, 0), (0, 2048)))
    gain_chains = []

    def early(block):
        part = product(after(gain_parts, block), (up_weights[0], up_weights[0]), PLAIN)[0]
        gain_chains.append(Chain(summed_over_features(jnp.sum(part, axis=0, keepdims=True))))
        return gain_chains[0]

    wides = [x.astype(F32) for x in (first_in, first_stash)]
    sums = both_z(jnp.concatenate([moments(w) for w in wides], axis=-1))
    _, _, forward_rows = normalize(wides[0], sums[:, 0:2], gain)
    normed, inverse_scale, backward_rows = normalize(wides[1], sums[:, 2:4], gain)

    later = lax.optimization_barrier(((stashed[1, 0], new_batch, new_grads), forward_rows))[0]
    late_core = kernel_call(copy_kernel, 1, ((8, 128), jnp.int32), awaited=(forward_rows,))(
        jnp.full((8, 128), core, jnp.int32)
    )[0][0, 0]
    second_stash, fresh_in, fresh_grad = [all_features(v, late_core) for v in later]
    wide = second_stash.astype(F32)
    normed_2, inverse_scale_2, backward_rows_2 = normalize(wide, both_z(moments(wide)), gain)

    gathered = Chain(gathering(backward_rows_2[None], (*Z_STEPS, *Y_STEPS)))
    forward_sum, grad_hidden = tick(
        jnp.stack([backward_rows, first_grad]),
        forward_rows,
        lambda block, multiply: (multiply(block[0], up, PLAIN), multiply(block[1], down, CONTRACT)),
        (),
        early,
        [gathered],
        up,
        down,
    )
    early_out = (wides[0] + forward_sum[:, :4096]).astype(BF)
    early_grad = gradient(grad_hidden, first_grad, normed, inverse_scale, gain)
    stored_part, stored_sent = product(gathered.result[0], up, PLAIN)

    passed_out, passed_grad = lax.optimization_barrier((early_out, early_grad))
    passed_out, passed_grad = passed_along(passed_out, 1), passed_along(passed_grad, -1)
    passed_out = after(passed_out, passed_grad)
    later_input = jnp.where(section == 0, fresh_in, passed_out)
    later_incoming = jnp.where(section == 3, fresh_grad, passed_grad)
    wide = later_input.astype(F32)
    _, _, forward_rows_2 = normalize(wide, after(both_z(moments(wide)), gathered.result), gain)
    forward_sum, grad_hidden = tick(
        later_incoming[None],
        forward_rows_2,
        lambda block, multiply: (multiply(block[0], down, CONTRACT),),
        (stored_part, stored_sent),
        lambda block: gain_chains[0],
        [],
        up,
        down,
    )
    later_out = (wide + forward_sum[:, :4096]).astype(BF)
    later_grad = gradient(grad_hidden, later_incoming, normed_2, inverse_scale_2, gain)

    def returned(early, later):
        both = jnp.stack([early, later])
        here = both[:, :, :2048]
        there = swap(both[:, :, 2048:], ACROSS_CORE)
        low = jnp.where(core == 0, here, there)
        high = jnp.where(core == 0, there, here)
        return jnp.concatenate([low, high], axis=1)[:, None]

    return returned(early_out, later_out), returned(early_grad, later_grad)


def solution(mesh):
    return jax.shard_map(
        shards,
        mesh=mesh,
        in_specs=(
            P("section", "tensor", "dp"),
            P("tensor", "dp"),
            P(None, "section", "tensor", "dp"),
            P("section", "tensor", "dp"),
            P("tensor", "dp"),
            P("section", "dp"),
            P("section", "dp", "tensor"),
            P("section", "tensor", "dp"),
        ),
        out_specs=(P(None, "section", "tensor", "dp"), P(None, "section", "tensor", "dp")),
        check_vma=False,
    )
```
